128 devices in a mesh: dp: 2 (over z_hi), expert: 64 (over x, y, z_lo, core).
Axes of the slice: x: 4, y: 4, z: 4 (z_hi: 2, z_lo: 2; z = z_hi * 2 + z_lo), core: 2. Of those that a mesh axis runs over, the one named last changes fastest.
Arguments:
- tokens: bfloat16 [8192, 2048], P('expert'), may hold values from -6 to 6
- routing: int32 [8192, 8], P('expert'), may hold values from 0 to 127, all different within a row; in each aligned block of 128 rows (0 to 127, 128 to 255, ...) at most 12 rows name the same one
- route_gates: float32 [8192, 8], P('expert'), may hold values from 0.03 to 0.3
- gate_weight: bfloat16 [128, 2048, 768], P('expert', None, 'dp'), may hold values from -0.125 to 0.125
- up_weight: bfloat16 [128, 2048, 768], P('expert', None, 'dp'), may hold values from -0.125 to 0.125
- down_weight: bfloat16 [128, 2048, 768], P('expert', None, 'dp'), may hold values from -0.21875 to 0.21875
- cotangent: bfloat16 [8192, 2048], P('expert'), may hold values from -4 to 4
Outputs:
- mixed: bfloat16 [8192, 2048], P('expert', 'dp')
- token_grad: bfloat16 [8192, 2048], P('expert', 'dp')
- gates_grad: float32 [8192, 8], P('expert')
- gate_grad: bfloat16 [128, 2048, 768], P('expert', None, 'dp')
- up_grad: bfloat16 [128, 2048, 768], P('expert', None, 'dp')
- down_grad: bfloat16 [128, 2048, 768], P('expert', None, 'dp')
The draws below stay inside these ranges and needn't reach their ends.
Inputs may be any that keep to these rules, and one draw needn't show every extreme that they name: `routing`: each row names 8 different experts. Among the rows of one index of expert (aligned blocks of 128 rows) no expert is named more than 12 times, a bound that some block reaches.
All inputs are finite; a program needn't handle non-finite values.
Results may differ from the reference program's by a relative error of at most 0.012.
Values may be sent and summed in bfloat16 or wider, within the bound.
No kernel may reach another device: no remote copies, remote signals or barrier semaphores. Data moves between devices by JAX's collectives and lax.ppermute only.
A program may use at most 192 MiB of HBM per device.

```python
import math
import jax
import jax.numpy as jnp
import numpy as np
from jax import lax

D = 2048
FF = 768
TOPK = 8
TOK_DEV = 128
EXPERTS = 128
TOKENS = 8192
CAP = 12
N_EXPERT = 64


def steps_of(rng, shape, cuts, smallest, high):
    factor_of = 1.0
    for dim, shards_of in cuts:
        steps = jax.random.uniform(jax.random.fold_in(jax.random.fold_in(rng, 6), dim), (shards_of,), jnp.float32, smallest / len(cuts), high / len(cuts))
        factor_of = factor_of * jnp.repeat(jnp.exp(steps), shape[dim] // shards_of).reshape((-1,) + (1,) * (len(shape) - 1 - dim))
    return factor_of


def deal_out(key, own, number, rows, number_of, top, most, lean):
    sequence = jax.random.permutation(key, number_of)
    crowded, common = shares(number_of, rows * top, most, lean, True), shares(number_of, rows * top, most, lean, False)
    places = jnp.arange(number_of)

    def named(tallies, rotation):
        used = int((tallies > 0).sum())
        fixed = max(1, used // 4)
        moved = fixed + (places - fixed + rotation * (used - fixed)) % max(1, number_of - fixed)
        return jnp.zeros((number_of,), jnp.int32).at[sequence[jnp.where(places < fixed, places, moved)]].set(jnp.asarray(tallies, jnp.int32))

    tallies = jnp.where(number % 4 == 0, named(crowded, number // 4), named(common, number - number // 4 - 1))
    mixed = jax.random.permutation(jax.random.fold_in(own, 3), number_of)
    source_of, taker = mixed[0:number_of // 2 * 2:2], mixed[1:number_of // 2 * 2:2]
    room = jnp.minimum(tallies[source_of] - 1, most - tallies[taker]) // 2
    room = jnp.where((source_of == sequence[0]) | (taker == sequence[0]) | (tallies[taker] == 0), 0, jnp.maximum(room, 0))
    moved = jax.random.randint(jax.random.fold_in(own, 4), (number_of // 2,), 0, 1 << 20) % (room + 1)
    tallies = tallies.at[source_of].add(-moved).at[taker].add(moved)
    members = jnp.searchsorted(jnp.cumsum(tallies), jnp.arange(rows * top), side="right").astype(jnp.int32)
    grid = members.reshape(top, rows).T
    grid = grid[jax.random.permutation(jax.random.fold_in(own, 1), rows)]
    rotation = jax.random.randint(jax.random.fold_in(own, 2), (rows, 1), 0, top)
    return jnp.take_along_axis(grid, (jnp.arange(top)[None, :] + rotation) % top, axis=1)


def shares(count, total, limit, skew, full):
    weights = [(1 << 20) // math.isqrt(grade ** skew) + 1 for grade in range(1, count + 1)]
    largest = limit if full else min(limit, max(-(-total // count), total * weights[0] // sum(weights)))
    least = 1 if total - largest >= count - 1 else 0
    holding, rest = [largest] + [least] * (count - 1), total - largest - least * (count - 1)
    while rest > 0:
        candidates = [i for i in range(1, count) if holding[i] < largest] or [i for i in range(1, count) if holding[i] < limit]
        whole, budget = sum([weights[i] for i in candidates]), rest
        for i in candidates:
            more = min(limit - holding[i], max(1, budget * weights[i] // whole), rest)
            holding[i] = holding[i] + more
            rest = rest - more
    return np.array(holding)


def centred(key, extent, scale, limit, cuts=(), kind=jnp.bfloat16):
    loudness = steps_of(key, extent, cuts, -0.22, 0.18) if cuts else 1.0
    values = jax.random.normal(key, extent, jnp.float32) * scale * loudness
    return jnp.minimum(jnp.maximum(values, -limit), limit).astype(kind)


def setup_inputs(seed: int = 0) -> dict:
    seeds = jax.random.split(jax.random.key(seed), 8)
    tokens = centred(seeds[0], (TOKENS, D), 1.0, 6.0, ((0, 64),))
    routing_keys = jax.random.split(jax.random.fold_in(seeds[1], 1), TOKENS // TOK_DEV)
    routing_turns = jax.random.permutation(jax.random.fold_in(seeds[1], 3), TOKENS // TOK_DEV)
    routing = jax.vmap(lambda own, number: deal_out(jax.random.fold_in(seeds[1], 2), own, number, TOK_DEV, EXPERTS, TOPK, CAP, 2))(routing_keys, routing_turns).reshape((TOKENS, TOPK))
    route_gates = jnp.clip(jnp.exp(math.log(0.3) - 2.3025852 * jax.random.uniform(seeds[2], (TOKENS, TOPK), jnp.float32) ** steps_of(seeds[2], (TOKENS, TOPK), ((0, 64),), -0.2, 0.2)), 0.03, 0.3)
    gate_weight = centred(seeds[3], (EXPERTS, D, FF), D ** -0.5, 0.125, ((0, 64), (2, 2)))
    up_weight = centred(seeds[4], (EXPERTS, D, FF), D ** -0.5, 0.125, ((0, 64), (2, 2)))
    down_weight = centred(seeds[5], (EXPERTS, D, FF), FF ** -0.5, 0.21875, ((0, 64), (2, 2)))
    cotangent = centred(seeds[6], (TOKENS, D), 0.5, 4.0, ((0, 64),))
    return {"tokens": tokens, "routing": routing, "route_gates": route_gates, "gate_weight": gate_weight, "up_weight": up_weight, "down_weight": down_weight, "cotangent": cotangent}


def expert_pass(slot_rows, slot_probs, slot_dout, w_gate, w_up, w_down):
    gate_pre = jnp.dot(slot_rows, w_gate, preferred_element_type=jnp.float32)
    up_pre = jnp.dot(slot_rows, w_up, preferred_element_type=jnp.float32)
    sigmoid_gate = jax.nn.sigmoid(gate_pre)
    active = gate_pre * sigmoid_gate
    hidden = (active * up_pre).astype(jnp.bfloat16)
    output = jnp.dot(hidden, w_down.T, preferred_element_type=jnp.float32).astype(jnp.bfloat16)
    slot_back = (slot_probs[:, None] * slot_dout.astype(jnp.float32)).astype(jnp.bfloat16)
    dhidden = jnp.dot(slot_back, w_down, preferred_element_type=jnp.float32)
    d_gate = (dhidden * up_pre * sigmoid_gate * (1.0 + gate_pre * (1.0 - sigmoid_gate))).astype(jnp.bfloat16)
    d_up = (dhidden * active).astype(jnp.bfloat16)
    row_grad = jnp.dot(d_gate, w_gate.T, preferred_element_type=jnp.float32)
    row_grad = (row_grad + jnp.dot(d_up, w_up.T, preferred_element_type=jnp.float32)).astype(jnp.bfloat16)
    grad_g = jnp.dot(slot_rows.T, d_gate, preferred_element_type=jnp.float32).astype(jnp.bfloat16)
    grad_u = jnp.dot(slot_rows.T, d_up, preferred_element_type=jnp.float32).astype(jnp.bfloat16)
    grad_d = jnp.dot(slot_back.T, hidden, preferred_element_type=jnp.float32).astype(jnp.bfloat16)
    return output, row_grad, grad_g, grad_u, grad_d


def reference(tokens, routing, route_gates, gate_weight, up_weight, down_weight, cotangent):
    blocks = N_EXPERT
    per_block = TOK_DEV * TOPK
    chosen = routing.reshape(blocks, per_block).astype(jnp.int32)
    one_hot = (chosen[:, :, None] == jnp.arange(EXPERTS, dtype=jnp.int32)[None, None, :]).astype(jnp.int32)
    running = jnp.cumsum(one_hot, axis=1) - one_hot
    within = jnp.sum(running * one_hot, axis=2).astype(jnp.int32)
    position = (jnp.arange(blocks, dtype=jnp.int32)[:, None] * CAP + within).astype(jnp.int32)
    assigned = jnp.arange(blocks * per_block, dtype=jnp.int32).reshape(blocks, per_block)
    table = jnp.full((EXPERTS, blocks * CAP), -1, jnp.int32).at[chosen, position].set(assigned)
    flat_gates = route_gates.reshape(-1)

    def one_expert(expert):
        ids = table[expert]
        valid = ids >= 0
        safe = jnp.maximum(ids, 0).astype(jnp.int32)
        source = (safe // TOPK).astype(jnp.int32)
        slot_rows = jnp.where(valid[:, None], tokens[source], jnp.zeros((), jnp.bfloat16))
        slot_probs = jnp.where(valid, flat_gates[safe], jnp.zeros((), jnp.float32))
        slot_dout = jnp.where(valid[:, None], cotangent[source], jnp.zeros((), jnp.bfloat16))
        return expert_pass(slot_rows, slot_probs, slot_dout,
                           gate_weight[expert], up_weight[expert], down_weight[expert])

    outputs, row_grads, gate_grad, up_grad, down_grad = lax.map(one_expert, jnp.arange(EXPERTS, dtype=jnp.int32))
    expert_rows = outputs[chosen, position].reshape(TOKENS, TOPK, D)
    grad_rows = row_grads[chosen, position].reshape(TOKENS, TOPK, D)
    expert_f = expert_rows.astype(jnp.float32)
    mixed = jnp.einsum('tk,tkd->td', route_gates, expert_f).astype(jnp.bfloat16)
    gates_grad = jnp.einsum('td,tkd->tk', cotangent.astype(jnp.float32), expert_f)
    token_grad = jnp.sum(grad_rows.astype(jnp.float32), axis=1).astype(jnp.bfloat16)
    return mixed, token_grad, gates_grad, gate_grad, up_grad, down_grad
```

```python
import functools

import jax
import jax.numpy as jnp
from jax import lax
from jax.experimental import pallas as pl
from jax.experimental.pallas import tpu as pltpu
from jax.sharding import PartitionSpec as P

BF = jnp.bfloat16
F32 = jnp.float32
TN = (((0,), (0,)), ((), ()))
NT = (((1,), (1,)), ((), ()))
LIMIT = 48 * 2**20


def dot(a, b, dims=(((1,), (0,)), ((), ())), precision=None):
    return lax.dot_general(a, b, dims, precision=precision, preferred_element_type=F32)


def iota(shape, dim):
    return lax.broadcasted_iota(jnp.int32, shape, dim)


def slot_experts(first, rows, experts, capacity):
    slot = first + iota((rows, experts), 0)
    low = iota((rows, experts), 1) * capacity
    return (slot >= low) & (slot < low + capacity)


def pack_rows_kernel(capacity, picks_ref, tokens_ref, rows_ref, place_ref, rank_ref):
    step = pl.program_id(0)
    experts, toks = rank_ref.shape
    rows = rows_ref.shape[0]

    @pl.when(step == 0)
    def _():
        named = jnp.zeros((experts, toks), F32)
        for k in range(picks_ref.shape[0]):
            named += (iota((experts, toks), 0) == picks_ref[k : k + 1, :]).astype(F32)
        before = (iota((toks, toks), 0) < iota((toks, toks), 1)).astype(F32).astype(BF)
        rank = dot(named.astype(BF), before)
        rank_ref[...] = jnp.where(named > 0, rank, -1.0).astype(BF)

    first = step * rows
    chosen = slot_experts(first, rows, experts, capacity).astype(F32).astype(BF)
    slot = (first + iota((rows, toks), 0)).astype(F32)
    within = slot - capacity * jnp.floor((slot + 0.5) * (1.0 / capacity))
    place = (dot(chosen, rank_ref[...]) == within).astype(F32).astype(BF)
    place_ref[...] = place
    rows_ref[...] = dot(place, tokens_ref[...]).astype(BF)


def pack_rows(picks, tokens, capacity, experts, steps=4):
    toks, width = tokens.shape
    slots = experts * capacity
    rows = slots // steps
    return pl.pallas_call(
        functools.partial(pack_rows_kernel, capacity),
        grid=(steps,),
        in_specs=[
            pl.BlockSpec(picks.shape, lambda i: (0, 0)),
            pl.BlockSpec((toks, width), lambda i: (0, 0)),
        ],
        out_specs=[
            pl.BlockSpec((rows, width), lambda i: (i, 0)),
            pl.BlockSpec((rows, toks), lambda i: (i, 0)),
        ],
        out_shape=[
            jax.ShapeDtypeStruct((slots, width), BF),
            jax.ShapeDtypeStruct((slots, toks), BF),
        ],
        scratch_shapes=[pltpu.VMEM((experts, toks), BF)],
        compiler_params=pltpu.CompilerParams(vmem_limit_bytes=LIMIT),
        cost_estimate=pl.CostEstimate(
            flops=2 * slots * toks * width, bytes_accessed=2 * slots * width, transcendentals=0
        ),
        name="pack_rows",
    )(picks, tokens)


def pack_back_kernel(capacity, picks_ref, gates_ref, place_ref, cot_ref, rows_ref, high_ref, low_ref, by_ref):
    step = pl.program_id(0)
    experts, toks = by_ref.shape
    rows = rows_ref.shape[0]

    @pl.when(step == 0)
    def _():
        by = jnp.zeros((experts, toks), F32)
        for k in range(picks_ref.shape[0]):
            by += jnp.where(iota((experts, toks), 0) == picks_ref[k : k + 1, :], gates_ref[k : k + 1, :], 0.0)
        by_ref[...] = by

    chosen = slot_experts(step * rows, rows, experts, capacity).astype(F32)
    place = place_ref[...]
    weight = place.astype(F32) * dot(chosen, by_ref[...], precision=lax.Precision.HIGHEST)
    high = weight.astype(BF)
    high_ref[...] = high
    low_ref[...] = (weight - high.astype(F32)).astype(BF)
    scale = jnp.sum(weight, axis=1, keepdims=True)
    rows_ref[...] = (scale * dot(place, cot_ref[...])).astype(BF)


def pack_back(picks, gates, place, cot, capacity, experts, steps=4):
    toks, width = cot.shape
    slots = experts * capacity
    rows = slots // steps
    whole = lambda i: (0, 0)
    part = lambda i: (i, 0)
    return pl.pallas_call(
        functools.partial(pack_back_kernel, capacity),
        grid=(steps,),
        in_specs=[
            pl.BlockSpec(picks.shape, whole),
            pl.BlockSpec(gates.shape, whole),
            pl.BlockSpec((rows, toks), part),
            pl.BlockSpec((toks, width), whole),
        ],
        out_specs=[
            pl.BlockSpec((rows, width), part),
            pl.BlockSpec((rows, toks), part),
            pl.BlockSpec((rows, toks), part),
        ],
        out_shape=[
            jax.ShapeDtypeStruct((slots, width), BF),
            jax.ShapeDtypeStruct((slots, toks), BF),
            jax.ShapeDtypeStruct((slots, toks), BF),
        ],
        scratch_shapes=[pltpu.VMEM((experts, toks), F32)],
        compiler_params=pltpu.CompilerParams(vmem_limit_bytes=LIMIT),
        cost_estimate=pl.CostEstimate(
            flops=2 * slots * toks * width, bytes_accessed=2 * slots * width, transcendentals=0
        ),
        name="pack_back",
    )(picks, gates, place, cot)


def mix_kernel(capacity, experts, picks_ref, place_ref, high_ref, low_ref, cot_ref, rows_ref, mixed_ref, gates_ref, along_ref):
    step = pl.program_id(0)
    rows = rows_ref[...]
    mixed_ref[...] = dot(high_ref[...], rows, TN) + dot(low_ref[...], rows, TN)
    along = dot(rows, cot_ref[...], NT)

    @pl.when(step == 0)
    def _():
        along_ref[...] = along

    @pl.when(step > 0)
    def _():
        along_ref[...] += along

    @pl.when(step == pl.num_programs(0) - 1)
    def _():
        slots, toks = along_ref.shape
        chosen = slot_experts(0, slots, experts, capacity).astype(F32)
        kept = along_ref[...] * place_ref[...].astype(F32)
        by = dot(chosen, kept, TN, precision=lax.Precision.HIGHEST)
        for k in range(picks_ref.shape[0]):
            mine = jnp.where(iota((experts, toks), 0) == picks_ref[k : k + 1, :], by, 0.0)
            gates_ref[k : k + 1, :] = jnp.sum(mine, axis=0, keepdims=True)


def mix(picks, place, high, low, cot, rows, capacity, experts, steps=4):
    toks, width = cot.shape
    slots = experts * capacity
    cols = width // steps
    whole = lambda i: (0, 0)
    part = lambda i: (0, i)
    return pl.pallas_call(
        functools.partial(mix_kernel, capacity, experts),
        grid=(steps,),
        in_specs=[
            pl.BlockSpec(picks.shape, whole),
            pl.BlockSpec((slots, toks), whole),
            pl.BlockSpec((slots, toks), whole),
            pl.BlockSpec((slots, toks), whole),
            pl.BlockSpec((toks, cols), part),
            pl.BlockSpec((slots, cols), part),
        ],
        out_specs=[pl.BlockSpec((toks, cols), part), pl.BlockSpec(picks.shape, whole)],
        out_shape=[
            jax.ShapeDtypeStruct((toks, width), F32),
            jax.ShapeDtypeStruct(picks.shape, F32),
        ],
        scratch_shapes=[pltpu.VMEM((slots, toks), F32)],
        compiler_params=pltpu.CompilerParams(vmem_limit_bytes=LIMIT),
        cost_estimate=pl.CostEstimate(
            flops=6 * slots * toks * width, bytes_accessed=2 * slots * width, transcendentals=0
        ),
        name="mix",
    )(picks, place, high, low, cot, rows)


def sum_rows_kernel(place_ref, rows_ref, out_ref):
    out_ref[...] = dot(place_ref[...], rows_ref[...], TN)


def sum_rows(place, rows, steps=4):
    slots, toks = place.shape
    width = rows.shape[1]
    cols = width // steps
    return pl.pallas_call(
        sum_rows_kernel,
        grid=(steps,),
        in_specs=[
            pl.BlockSpec((slots, toks), lambda i: (0, 0)),
            pl.BlockSpec((slots, cols), lambda i: (0, i)),
        ],
        out_specs=pl.BlockSpec((toks, cols), lambda i: (0, i)),
        out_shape=jax.ShapeDtypeStruct((toks, width), F32),
        compiler_params=pltpu.CompilerParams(vmem_limit_bytes=LIMIT),
        cost_estimate=pl.CostEstimate(
            flops=2 * slots * toks * width, bytes_accessed=2 * slots * width, transcendentals=0
        ),
        name="sum_rows",
    )(place, rows)


def exchange(rows):
    return lax.all_to_all(rows, "expert", split_axis=0, concat_axis=0, tiled=True)


def other(value):
    return lax.ppermute(value, "dp", [(0, 1), (1, 0)])


def add_over_dp(part):
    half = part.shape[1] // 2
    member = lax.axis_index("dp")
    away = lax.dynamic_slice_in_dim(part, (1 - member) * half, half, 1).astype(BF)
    kept = lax.dynamic_slice_in_dim(part, member * half, half, 1)
    return (kept + other(away).astype(F32)).astype(BF)


def body(tokens, routing, route_gates, gate_weight, up_weight, down_weight, cotangent):
    toks, width = tokens.shape
    local = gate_weight.shape[0]
    experts = local * lax.axis_size("expert")
    capacity = 3 * toks * routing.shape[1] // (2 * experts)
    slots = experts * capacity
    picks, gates = routing.T, route_gates.T

    sent_rows, place = pack_rows(picks, tokens, capacity, experts)
    x = exchange(sent_rows)
    sent_back, high, low = pack_back(picks, gates, place, cotangent, capacity, experts)
    back = exchange(sent_back)

    second = (iota((slots, 1), 0) // capacity) % local == 1

    def by_expert(rows, weight, dims=(((1,), (0,)), ((), ()))):
        return jnp.where(second, dot(rows, weight[1], dims), dot(rows, weight[0], dims))

    def halves(value):
        zero = jnp.zeros((), value.dtype)
        return jnp.where(second, zero, value), jnp.where(second, value, zero)

    gate_pre = by_expert(x, gate_weight)
    up_pre = by_expert(x, up_weight)
    s = jax.nn.sigmoid(gate_pre)
    active = gate_pre * s
    hidden = halves((active * up_pre).astype(BF))
    out = (dot(hidden[0], down_weight[0], NT) + dot(hidden[1], down_weight[1], NT)).astype(BF)
    back, out = lax.optimization_barrier((back, out))
    got_out = exchange(out)

    dhidden = by_expert(back, down_weight)
    d_gate = halves((dhidden * up_pre * s * (1.0 + gate_pre * (1.0 - s))).astype(BF))
    d_up = halves((dhidden * active).astype(BF))
    row = sum(
        dot(d_gate[j], gate_weight[j], NT) + dot(d_up[j], up_weight[j], NT) for j in range(local)
    ).astype(BF)
    row, got_out = lax.optimization_barrier((row, got_out))
    got_row = exchange(row)

    mixed_part, gates_part = mix(picks, place, high, low, cotangent, got_out, capacity, experts)
    mixed = add_over_dp(mixed_part)
    gates_grad = (gates_part + other(gates_part)).T
    token_grad = add_over_dp(sum_rows(place, got_row))

    def outer(rows, values):
        return jnp.stack([dot(rows, values[j], TN).astype(BF) for j in range(local)])

    return (
        mixed,
        token_grad,
        gates_grad,
        outer(x, d_gate),
        outer(x, d_up),
        outer(back, hidden),
    )


def solution(mesh):
    by_dp = P("expert", None, "dp")
    rows = P("expert", None)
    in_specs = (rows, rows, rows, by_dp, by_dp, by_dp, rows)
    out_specs = (P("expert", "dp"), P("expert", "dp"), rows, by_dp, by_dp, by_dp)
    return jax.shard_map(body, mesh=mesh, in_specs=in_specs, out_specs=out_specs, check_vma=False)
```

```python
import functools

import jax
import jax.numpy as jnp
from jax import lax
from jax.experimental import pallas as pl
from jax.experimental.pallas import tpu as pltpu
from jax.sharding import PartitionSpec as P

BF = jnp.bfloat16
F32 = jnp.float32
NN = (((1,), (0,)), ((), ()))
TN = (((0,), (0,)), ((), ()))
NT = (((1,), (1,)), ((), ()))
LIMIT = 48 * 2**20
PACK_LIMIT = 60 * 2**20
GROUP = 4
EXACT = lax.Precision.HIGHEST


def dot(a, b, dims=NN, precision=None):
    return lax.dot_general(a, b, dims, precision=precision, preferred_element_type=F32)


def iota(shape, dim):
    return lax.broadcasted_iota(jnp.int32, shape, dim)


def as_float(flags):
    return flags.astype(F32)


def slot_parts(first, rows, cols, capacity):
    slot = as_float(first + iota((rows, cols), 0))
    place = jnp.floor((slot + 0.5) * (1.0 / (GROUP * capacity)))
    rest = slot - GROUP * capacity * place
    block = jnp.floor((rest + 0.5) * (1.0 / capacity))
    return place, block, rest - capacity * block


def one_hot_pair(first, rows, places, capacity):
    place, block, _ = slot_parts(first, rows, GROUP * places, capacity)
    return as_float(as_float(iota((rows, GROUP * places), 1)) == block * places + place)


def by_pair(keys_ref, value, places, step=8.0):
    toks = keys_ref.shape[1]
    picks = keys_ref.shape[0] // GROUP
    wanted = as_float(iota((places, toks), 0)) * step
    blocks = []
    for b in range(GROUP):
        total = jnp.zeros((places, toks), F32)
        for k in range(picks):
            row = b * picks + k
            total += jnp.where(keys_ref[row : row + 1, :] == wanted, value(row), 0.0)
        blocks.append(total)
    return jnp.concatenate(blocks, axis=0)


def pack_rows_kernel(capacity, step_of, keys_ref, near_ref, far_ref, rows_ref, place_ref, rank_ref):
    step = pl.program_id(0)
    pairs, toks = rank_ref.shape
    places = pairs // GROUP
    rows = rows_ref.shape[0]

    @pl.when(step == 0)
    def _():
        named = by_pair(keys_ref, lambda row: 1.0, places, step_of)
        before = as_float(iota((toks, toks), 0) < iota((toks, toks), 1)).astype(BF)
        rank = dot(named.astype(BF), before)
        rank_ref[...] = jnp.where(named > 0, rank, -1.0).astype(BF)

    first = step * rows
    pair = one_hot_pair(first, rows, places, capacity).astype(BF)
    _, block, rank = slot_parts(first, rows, toks, capacity)
    hit = dot(pair, rank_ref[...]) == rank
    place = jnp.concatenate(
        [as_float(hit & (block == float(b))) for b in range(GROUP)], axis=1
    ).astype(BF)
    place_ref[...] = place
    half = near_ref.shape[0]
    rows_ref[...] = (
        dot(place[:, :half], near_ref[...]) + dot(place[:, half:], far_ref[...])
    ).astype(BF)


def pack_rows(keys, near, far, capacity, places, step_of, steps=2):
    toks = keys.shape[1]
    width = near.shape[1]
    slots = places * GROUP * capacity
    rows = slots // steps
    whole = lambda i: (0, 0)
    part = lambda i: (i, 0)
    return pl.pallas_call(
        functools.partial(pack_rows_kernel, capacity, step_of),
        grid=(steps,),
        in_specs=[pl.BlockSpec(a.shape, whole) for a in (keys, near, far)],
        out_specs=[
            pl.BlockSpec((rows, width), part),
            pl.BlockSpec((rows, GROUP * toks), part),
        ],
        out_shape=[
            jax.ShapeDtypeStruct((slots, width), BF),
            jax.ShapeDtypeStruct((slots, GROUP * toks), BF),
        ],
        scratch_shapes=[pltpu.VMEM((GROUP * places, toks), BF)],
        compiler_params=pltpu.CompilerParams(vmem_limit_bytes=PACK_LIMIT),
        cost_estimate=pl.CostEstimate(
            flops=8 * slots * toks * width, bytes_accessed=2 * slots * width, transcendentals=0
        ),
        name="pack_rows",
    )(keys, near, far)


def pack_back_kernel(capacity, step_of, keys_ref, gates_ref, place_ref, near_ref, far_ref, rows_ref, high_ref, low_ref, by_ref):
    step = pl.program_id(0)
    pairs, toks = by_ref.shape
    places = pairs // GROUP
    rows = rows_ref.shape[0]

    @pl.when(step == 0)
    def _():
        by_ref[...] = by_pair(keys_ref, lambda row: gates_ref[row : row + 1, :], places, step_of)

    pair = one_hot_pair(step * rows, rows, places, capacity)
    gate = dot(pair, by_ref[...], precision=EXACT)
    place = place_ref[...]
    weight = as_float(place) * jnp.concatenate([gate] * GROUP, axis=1)
    high = weight.astype(BF)
    high_ref[...] = high
    low_ref[...] = (weight - as_float(high)).astype(BF)
    scale = jnp.sum(weight, axis=1, keepdims=True)
    half = near_ref.shape[0]
    cot = dot(place[:, :half], near_ref[...]) + dot(place[:, half:], far_ref[...])
    rows_ref[...] = (scale * cot).astype(BF)


def pack_back(keys, gates, place, near, far, capacity, places, step_of, steps=2):
    toks = keys.shape[1]
    width = near.shape[1]
    slots = places * GROUP * capacity
    rows = slots // steps
    whole = lambda i: (0, 0)
    part = lambda i: (i, 0)
    return pl.pallas_call(
        functools.partial(pack_back_kernel, capacity, step_of),
        grid=(steps,),
        in_specs=[
            pl.BlockSpec(keys.shape, whole),
            pl.BlockSpec(gates.shape, whole),
            pl.BlockSpec((rows, GROUP * toks), part),
            pl.BlockSpec(near.shape, whole),
            pl.BlockSpec(far.shape, whole),
        ],
        out_specs=[
            pl.BlockSpec((rows, width), part),
            pl.BlockSpec((rows, GROUP * toks), part),
            pl.BlockSpec((rows, GROUP * toks), part),
        ],
        out_shape=[
            jax.ShapeDtypeStruct((slots, width), BF),
            jax.ShapeDtypeStruct((slots, GROUP * toks), BF),
            jax.ShapeDtypeStruct((slots, GROUP * toks), BF),
        ],
        scratch_shapes=[pltpu.VMEM((GROUP * places, toks), F32)],
        compiler_params=pltpu.CompilerParams(vmem_limit_bytes=PACK_LIMIT),
        cost_estimate=pl.CostEstimate(
            flops=8 * slots * toks * width, bytes_accessed=2 * slots * width, transcendentals=0
        ),
        name="pack_back",
    )(keys, gates, place, near, far)


def mix_kernel(capacity, places, step_of, keys_ref, place_ref, high_ref, low_ref, near_ref, far_ref, rows_ref, kept_ref, sent_ref, gates_ref, along_ref):
    step = pl.program_id(0)
    rows = rows_ref[...]
    half = near_ref.shape[0]
    mixed = dot(high_ref[...], rows, TN) + dot(low_ref[...], rows, TN)
    kept_ref[...] = mixed[:half]
    sent_ref[...] = mixed[half:].astype(BF)

    @pl.when(step == 0)
    def _():
        along_ref[...] = jnp.zeros_like(along_ref)

    along_ref[:, :half] += dot(rows, near_ref[...], NT)
    along_ref[:, half:] += dot(rows, far_ref[...], NT)

    @pl.when(step == pl.num_programs(0) - 1)
    def _():
        slots = along_ref.shape[0]
        toks = keys_ref.shape[1]
        picks = keys_ref.shape[0] // GROUP
        kept = along_ref[...] * as_float(place_ref[...])
        kept = sum(kept[:, b * toks : (b + 1) * toks] for b in range(GROUP))
        by = dot(one_hot_pair(0, slots, places, capacity), kept, TN, precision=EXACT)
        wanted = as_float(iota((places, toks), 0)) * step_of
        for b in range(GROUP):
            mine = by[b * places : (b + 1) * places, :]
            for k in range(picks):
                row = b * picks + k
                chosen = jnp.where(keys_ref[row : row + 1, :] == wanted, mine, 0.0)
                gates_ref[row : row + 1, :] = jnp.sum(chosen, axis=0, keepdims=True)


def mix(keys, place, high, low, near, far, rows, capacity, places, step_of, steps=4):
    slots, all_toks = place.shape
    width = rows.shape[1]
    cols = width // steps
    whole = lambda i: (0, 0)
    part = lambda i: (0, i)
    return pl.pallas_call(
        functools.partial(mix_kernel, capacity, places, step_of),
        grid=(steps,),
        in_specs=[pl.BlockSpec(a.shape, whole) for a in (keys, place, high, low)]
        + [pl.BlockSpec((a.shape[0], cols), part) for a in (near, far, rows)],
        out_specs=[pl.BlockSpec((all_toks // 2, cols), part)] * 2 + [pl.BlockSpec(keys.shape, whole)],
        out_shape=[
            jax.ShapeDtypeStruct((all_toks // 2, width), F32),
            jax.ShapeDtypeStruct((all_toks // 2, width), BF),
            jax.ShapeDtypeStruct(keys.shape, F32),
        ],
        scratch_shapes=[pltpu.VMEM((slots, all_toks), F32)],
        compiler_params=pltpu.CompilerParams(vmem_limit_bytes=LIMIT),
        cost_estimate=pl.CostEstimate(
            flops=6 * slots * all_toks * width, bytes_accessed=2 * slots * width, transcendentals=0
        ),
        name="mix",
    )(keys, place, high, low, near, far, rows)


def sum_rows_kernel(place_ref, rows_ref, kept_ref, sent_ref):
    total = dot(place_ref[...], rows_ref[...], TN)
    half = kept_ref.shape[0]
    kept_ref[...] = total[:half]
    sent_ref[...] = total[half:].astype(BF)


def sum_rows(place, rows, steps=4):
    slots, toks = place.shape
    width = rows.shape[1]
    cols = width // steps
    return pl.pallas_call(
        sum_rows_kernel,
        grid=(steps,),
        in_specs=[
            pl.BlockSpec((slots, toks), lambda i: (0, 0)),
            pl.BlockSpec((slots, cols), lambda i: (0, i)),
        ],
        out_specs=[pl.BlockSpec((toks // 2, cols), lambda i: (0, i))] * 2,
        out_shape=[
            jax.ShapeDtypeStruct((toks // 2, width), F32),
            jax.ShapeDtypeStruct((toks // 2, width), BF),
        ],
        compiler_params=pltpu.CompilerParams(vmem_limit_bytes=LIMIT),
        cost_estimate=pl.CostEstimate(
            flops=2 * slots * toks * width, bytes_accessed=2 * slots * width, transcendentals=0
        ),
        name="sum_rows",
    )(place, rows)


def exchange(rows, devices):
    groups = [list(range(g, devices, GROUP)) for g in range(GROUP)]
    return lax.all_to_all(
        rows, "expert", split_axis=0, concat_axis=0, tiled=True, axis_index_groups=groups
    )


def swap(value, devices, across=0, within=0):
    pairs = [
        (m * devices + s, (m ^ across) * devices + (s ^ within)) for m in range(2) for s in range(devices)
    ]
    return lax.ppermute(value, ("dp", "expert"), pairs)


CORE, Z = 1, 2


def body(tokens, routing, route_gates, gate_weight, up_weight, down_weight, cotangent):
    toks, width = tokens.shape
    picks = routing.shape[1]
    local = gate_weight.shape[0]
    devices = lax.axis_size("expert")
    experts = local * devices
    capacity = 3 * toks * picks // (2 * experts)
    places = devices // GROUP
    step_of = float(local * GROUP)
    half = width // 2
    member = lax.axis_index("dp")
    swapped = functools.partial(swap, devices=devices)

    def mine(value, size, dim, flip=False):
        index = 1 - member if flip else member
        return lax.dynamic_slice_in_dim(value, index * size, size, dim)

    def after(value, *others):
        return lax.optimization_barrier((value, *others))[0]

    def kept_half(weight):
        return mine(weight, 1, 0)[0]

    def in_pieces(sent, pieces):
        size = sent.shape[0] // pieces
        return [swapped(sent[i * size : (i + 1) * size], across=1) for i in range(pieces)]

    def got_half(weight, pieces):
        return in_pieces(mine(weight, 1, 0, flip=True)[0], pieces)

    gate_pieces = got_half(gate_weight, 4)
    up_pieces = got_half(up_weight, 2)
    w_gate = kept_half(gate_weight), jnp.concatenate(gate_pieces)
    w_up = kept_half(up_weight), jnp.concatenate(up_pieces)
    w_down = kept_half(down_weight), got_half(down_weight, 1)[0]

    def z_rows(columns, across):
        return swapped(jnp.concatenate([tokens[:, columns], cotangent[:, columns]]), across=across, within=Z)

    table = jnp.concatenate([routing.T.astype(F32), route_gates.T], axis=0)
    near_table = jnp.stack([table, swapped(table, within=Z)])
    left, right = z_rows(slice(0, half), 0), z_rows(slice(half, width), 1)
    near_x = jnp.concatenate([tokens, jnp.concatenate([left[:toks], right[:toks]], axis=1)])
    near_c = jnp.concatenate([cotangent, jnp.concatenate([left[toks:], right[toks:]], axis=1)])
    near_x = after(near_x, near_table, gate_pieces[0])
    far_x, far_c = swapped(near_x, within=CORE), swapped(near_c, within=CORE)
    all_tables = jnp.concatenate([near_table, swapped(near_table, within=CORE)], axis=0)
    offset = (lax.axis_index("expert") % GROUP) * local + member
    keys = all_tables[:, :picks].reshape(GROUP * picks, toks) - offset.astype(F32)
    gates = all_tables[:, picks:].reshape(GROUP * picks, toks)

    sent_rows, place = pack_rows(keys, near_x, far_x, capacity, places, step_of)
    x = exchange(after(sent_rows, gate_pieces[1]), devices)
    sent_back, high, low = pack_back(
        after(keys, *gate_pieces[2:]), gates, place, near_c, far_c, capacity, places, step_of
    )
    back = exchange(after(sent_back, up_pieces[0]), devices)
    x = after(x, up_pieces[1])

    hidden, saved = [], []
    for j in range(2):
        gate_pre = dot(x, w_gate[j])
        up_pre = dot(x, w_up[j])
        s = jax.nn.sigmoid(gate_pre)
        active = gate_pre * s
        hidden.append((active * up_pre).astype(BF))
        saved.append((gate_pre, up_pre, s, active))
    out = (dot(hidden[0], w_down[0], NT) + dot(hidden[1], w_down[1], NT)).astype(BF)

    def outer(rows, values):
        return dot(rows, values, TN).astype(BF)

    def inner(j, back):
        gate_pre, up_pre, s, active = saved[j]
        dhidden = dot(back, w_down[j])
        d_gate = (dhidden * up_pre * s * (1.0 + gate_pre * (1.0 - s))).astype(BF)
        return d_gate, (dhidden * active).astype(BF)

    def partner(value):
        return swapped(value, across=1)

    back = after(back, out)
    sent_down = outer(back, hidden[1])
    got_out = exchange(after(out, sent_down), devices)
    d_gate1, d_up1 = inner(1, after(back, sent_down))
    sent_gate, sent_up = outer(x, d_gate1), outer(x, d_up1)
    d_gate0, d_up0 = inner(0, after(back, sent_gate, sent_up))
    row = (
        dot(d_gate0, w_gate[0], NT)
        + dot(d_up0, w_up[0], NT)
        + dot(d_gate1, w_gate[1], NT)
        + dot(d_up1, w_up[1], NT)
    ).astype(BF)
    got_down, got_gate, got_up = partner(sent_down), partner(sent_gate), partner(sent_up)
    got_row = exchange(after(row, got_out, got_down), devices)

    def spread(kept, sent):
        kept = kept + swapped(sent, within=CORE).astype(F32)
        same, cross = mine(kept, half, 1), mine(kept, half, 1, flip=True)
        return same[:toks], [
            swapped(same[toks:].astype(BF), within=Z),
            swapped(cross[toks:].astype(BF), across=1, within=Z),
            swapped(cross[:toks].astype(BF), across=1),
        ]

    def collect(own, got):
        return (own + sum(g.astype(F32) for g in got)).astype(BF)

    def both(kept, got):
        first = iota((local, 1, 1), 0) == member
        return jnp.where(first, kept[None], got[None])

    mixed_kept, mixed_sent, gates_part = mix(
        keys, place, high, low, near_c, far_c, after(got_out, got_gate), capacity, places, step_of
    )
    down_grad = both(outer(after(back, mixed_kept), hidden[0]), got_down)
    gate_grad = both(outer(after(x, mixed_kept), d_gate0), got_gate)
    kept_up = outer(after(x, mixed_kept), d_up0)
    mixed_own, mixed_got = spread(mixed_kept, mixed_sent)
    mixed = collect(mixed_own, mixed_got)
    token_own, token_got = spread(*sum_rows(place, after(got_row, down_grad, gate_grad, kept_up)))
    token_grad = collect(token_own, token_got)
    up_grad = both(kept_up, after(got_up, token_grad))

    gates_near = gates_part[: 2 * picks] + swapped(gates_part[2 * picks :], within=CORE)
    own, away = gates_near[:picks], gates_near[picks:]
    gates_got = [partner(own), swapped(away, within=Z), swapped(away, across=1, within=Z)]
    gates_got = [after(g, token_own) for g in gates_got]
    gates_sum = (own + gates_got[0]) + (gates_got[1] + gates_got[2])
    return mixed, token_grad, gates_sum.T, gate_grad, up_grad, down_grad


def solution(mesh):
    by_dp = P("expert", None, "dp")
    rows = P("expert", None)
    in_specs = (rows, rows, rows, by_dp, by_dp, by_dp, rows)
    out_specs = (P("expert", "dp"), P("expert", "dp"), rows, by_dp, by_dp, by_dp)
    return jax.shard_map(body, mesh=mesh, in_specs=in_specs, out_specs=out_specs, check_vma=False)
```

```python
import functools

import jax
import jax.numpy as jnp
from jax import lax
from jax.experimental import pallas as pl
from jax.experimental.pallas import tpu as pltpu
from jax.sharding import PartitionSpec as P

BF = jnp.bfloat16
F32 = jnp.float32
NN = (((1,), (0,)), ((), ()))
TN = (((0,), (0,)), ((), ()))
NT = (((1,), (1,)), ((), ()))
LIMIT = 48 * 2**20
PACK_LIMIT = 60 * 2**20
GROUP = 4
EXACT = lax.Precision.HIGHEST


def dot(a, b, dims=NN, precision=None):
    return lax.dot_general(a, b, dims, precision=precision, preferred_element_type=F32)


def iota(shape, dim):
    return lax.broadcasted_iota(jnp.int32, shape, dim)


def as_float(flags):
    return flags.astype(F32)


def slot_parts(first, rows, cols, capacity):
    slot = as_float(first + iota((rows, cols), 0))
    place = jnp.floor((slot + 0.5) * (1.0 / (GROUP * capacity)))
    rest = slot - GROUP * capacity * place
    block = jnp.floor((rest + 0.5) * (1.0 / capacity))
    return place, block, rest - capacity * block


def one_hot_pair(first, rows, places, capacity):
    place, block, _ = slot_parts(first, rows, GROUP * places, capacity)
    return as_float(as_float(iota((rows, GROUP * places), 1)) == block * places + place)


def by_pair(keys_ref, value, places, step=8.0):
    toks = keys_ref.shape[1]
    picks = keys_ref.shape[0] // GROUP
    wanted = as_float(iota((places, toks), 0)) * step
    blocks = []
    for b in range(GROUP):
        total = jnp.zeros((places, toks), F32)
        for k in range(picks):
            row = b * picks + k
            total += jnp.where(keys_ref[row : row + 1, :] == wanted, value(row), 0.0)
        blocks.append(total)
    return jnp.concatenate(blocks, axis=0)


def pack_rows_kernel(capacity, step_of, keys_ref, near_ref, far_ref, rows_ref, place_ref, rank_ref):
    step = pl.program_id(0)
    pairs, toks = rank_ref.shape
    places = pairs // GROUP
    rows = rows_ref.shape[0]

    @pl.when(step == 0)
    def _():
        named = by_pair(keys_ref, lambda row: 1.0, places, step_of)
        before = as_float(iota((toks, toks), 0) < iota((toks, toks), 1)).astype(BF)
        rank = dot(named.astype(BF), before)
        rank_ref[...] = jnp.where(named > 0, rank, -1.0).astype(BF)

    first = step * rows
    pair = one_hot_pair(first, rows, places, capacity).astype(BF)
    _, block, rank = slot_parts(first, rows, toks, capacity)
    hit = dot(pair, rank_ref[...]) == rank
    place = jnp.concatenate(
        [as_float(hit & (block == float(b))) for b in range(GROUP)], axis=1
    ).astype(BF)
    place_ref[...] = place
    half = near_ref.shape[0]
    rows_ref[...] = (
        dot(place[:, :half], near_ref[...]) + dot(place[:, half:], far_ref[...])
    ).astype(BF)


def pack_rows(keys, near, far, capacity, places, step_of, steps=2):
    toks = keys.shape[1]
    width = near.shape[1]
    slots = places * GROUP * capacity
    rows = slots // steps
    whole = lambda i: (0, 0)
    part = lambda i: (i, 0)
    return pl.pallas_call(
        functools.partial(pack_rows_kernel, capacity, step_of),
        grid=(steps,),
        in_specs=[pl.BlockSpec(a.shape, whole) for a in (keys, near, far)],
        out_specs=[
            pl.BlockSpec((rows, width), part),
            pl.BlockSpec((rows, GROUP * toks), part),
        ],
        out_shape=[
            jax.ShapeDtypeStruct((slots, width), BF),
            jax.ShapeDtypeStruct((slots, GROUP * toks), BF),
        ],
        scratch_shapes=[pltpu.VMEM((GROUP * places, toks), BF)],
        compiler_params=pltpu.CompilerParams(vmem_limit_bytes=PACK_LIMIT),
        cost_estimate=pl.CostEstimate(
            flops=8 * slots * toks * width, bytes_accessed=2 * slots * width, transcendentals=0
        ),
        name="pack_rows",
    )(keys, near, far)


def pack_back_kernel(capacity, step_of, keys_ref, gates_ref, place_ref, near_ref, far_ref, rows_ref, high_ref, low_ref, by_ref):
    step = pl.program_id(0)
    pairs, toks = by_ref.shape
    places = pairs // GROUP
    rows = rows_ref.shape[0]

    @pl.when(step == 0)
    def _():
        by_ref[...] = by_pair(keys_ref, lambda row: gates_ref[row : row + 1, :], places, step_of)

    pair = one_hot_pair(step * rows, rows, places, capacity)
    gate = dot(pair, by_ref[...], precision=EXACT)
    place = place_ref[...]
    weight = as_float(place) * jnp.concatenate([gate] * GROUP, axis=1)
    high = weight.astype(BF)
    high_ref[...] = high
    low_ref[...] = (weight - as_float(high)).astype(BF)
    scale = jnp.sum(weight, axis=1, keepdims=True)
    half = near_ref.shape[0]
    cot = dot(place[:, :half], near_ref[...]) + dot(place[:, half:], far_ref[...])
    rows_ref[...] = (scale * cot).astype(BF)


def pack_back(keys, gates, place, near, far, capacity, places, step_of, steps=2):
    toks = keys.shape[1]
    width = near.shape[1]
    slots = places * GROUP * capacity
    rows = slots // steps
    whole = lambda i: (0, 0)
    part = lambda i: (i, 0)
    return pl.pallas_call(
        functools.partial(pack_back_kernel, capacity, step_of),
        grid=(steps,),
        in_specs=[
            pl.BlockSpec(keys.shape, whole),
            pl.BlockSpec(gates.shape, whole),
            pl.BlockSpec((rows, GROUP * toks), part),
            pl.BlockSpec(near.shape, whole),
            pl.BlockSpec(far.shape, whole),
        ],
        out_specs=[
            pl.BlockSpec((rows, width), part),
            pl.BlockSpec((rows, GROUP * toks), part),
            pl.BlockSpec((rows, GROUP * toks), part),
        ],
        out_shape=[
            jax.ShapeDtypeStruct((slots, width), BF),
            jax.ShapeDtypeStruct((slots, GROUP * toks), BF),
            jax.ShapeDtypeStruct((slots, GROUP * toks), BF),
        ],
        scratch_shapes=[pltpu.VMEM((GROUP * places, toks), F32)],
        compiler_params=pltpu.CompilerParams(vmem_limit_bytes=PACK_LIMIT),
        cost_estimate=pl.CostEstimate(
            flops=8 * slots * toks * width, bytes_accessed=2 * slots * width, transcendentals=0
        ),
        name="pack_back",
    )(keys, gates, place, near, far)


def mix_kernel(capacity, places, step_of, keys_ref, place_ref, high_ref, low_ref, near_ref, far_ref, rows_ref, kept_ref, sent_ref, gates_ref, along_ref):
    step = pl.program_id(0)
    rows = rows_ref[...]
    half = near_ref.shape[0]
    mixed = dot(high_ref[...], rows, TN) + dot(low_ref[...], rows, TN)
    kept_ref[...] = mixed[:half]
    sent_ref[...] = mixed[half:].astype(BF)

    @pl.when(step == 0)
    def _():
        along_ref[...] = jnp.zeros_like(along_ref)

    along_ref[:, :half] += dot(rows, near_ref[...], NT)
    along_ref[:, half:] += dot(rows, far_ref[...], NT)

    @pl.when(step == pl.num_programs(0) - 1)
    def _():
        slots = along_ref.shape[0]
        toks = keys_ref.shape[1]
        picks = keys_ref.shape[0] // GROUP
        kept = along_ref[...] * as_float(place_ref[...])
        kept = sum(kept[:, b * toks : (b + 1) * toks] for b in range(GROUP))
        by = dot(one_hot_pair(0, slots, places, capacity), kept, TN, precision=EXACT)
        wanted = as_float(iota((places, toks), 0)) * step_of
        for b in range(GROUP):
            mine = by[b * places : (b + 1) * places, :]
            for k in range(picks):
                row = b * picks + k
                chosen = jnp.where(keys_ref[row : row + 1, :] == wanted, mine, 0.0)
                gates_ref[row : row + 1, :] = jnp.sum(chosen, axis=0, keepdims=True)


def mix(keys, place, high, low, near, far, rows, capacity, places, step_of, steps=4):
    slots, all_toks = place.shape
    width = rows.shape[1]
    cols = width // steps
    whole = lambda i: (0, 0)
    part = lambda i: (0, i)
    return pl.pallas_call(
        functools.partial(mix_kernel, capacity, places, step_of),
        grid=(steps,),
        in_specs=[pl.BlockSpec(a.shape, whole) for a in (keys, place, high, low)]
        + [pl.BlockSpec((a.shape[0], cols), part) for a in (near, far, rows)],
        out_specs=[pl.BlockSpec((all_toks // 2, cols), part)] * 2 + [pl.BlockSpec(keys.shape, whole)],
        out_shape=[
            jax.ShapeDtypeStruct((all_toks // 2, width), F32),
            jax.ShapeDtypeStruct((all_toks // 2, width), BF),
            jax.ShapeDtypeStruct(keys.shape, F32),
        ],
        scratch_shapes=[pltpu.VMEM((slots, all_toks), F32)],
        compiler_params=pltpu.CompilerParams(vmem_limit_bytes=LIMIT),
        cost_estimate=pl.CostEstimate(
            flops=6 * slots * all_toks * width, bytes_accessed=2 * slots * width, transcendentals=0
        ),
        name="mix",
    )(keys, place, high, low, near, far, rows)


def sum_rows_kernel(place_ref, rows_ref, kept_ref, sent_ref):
    total = dot(place_ref[...], rows_ref[...], TN)
    half = kept_ref.shape[0]
    kept_ref[...] = total[:half]
    sent_ref[...] = total[half:].astype(BF)


def sum_rows(place, rows, steps=4):
    slots, toks = place.shape
    width = rows.shape[1]
    cols = width // steps
    return pl.pallas_call(
        sum_rows_kernel,
        grid=(steps,),
        in_specs=[
            pl.BlockSpec((slots, toks), lambda i: (0, 0)),
            pl.BlockSpec((slots, cols), lambda i: (0, i)),
        ],
        out_specs=[pl.BlockSpec((toks // 2, cols), lambda i: (0, i))] * 2,
        out_shape=[
            jax.ShapeDtypeStruct((toks // 2, width), F32),
            jax.ShapeDtypeStruct((toks // 2, width), BF),
        ],
        compiler_params=pltpu.CompilerParams(vmem_limit_bytes=LIMIT),
        cost_estimate=pl.CostEstimate(
            flops=2 * slots * toks * width, bytes_accessed=2 * slots * width, transcendentals=0
        ),
        name="sum_rows",
    )(place, rows)


def exchange(rows, devices):
    groups = [list(range(g, devices, GROUP)) for g in range(GROUP)]
    return lax.all_to_all(
        rows, "expert", split_axis=0, concat_axis=0, tiled=True, axis_index_groups=groups
    )


def swap(value, devices, across=0, within=0):
    pairs = [
        (m * devices + s, (m ^ across) * devices + (s ^ within)) for m in range(2) for s in range(devices)
    ]
    return lax.ppermute(value, ("dp", "expert"), pairs)


CORE, Z = 1, 2


def body(tokens, routing, route_gates, gate_weight, up_weight, down_weight, cotangent):
    toks, width = tokens.shape
    picks = routing.shape[1]
    local = gate_weight.shape[0]
    devices = lax.axis_size("expert")
    experts = local * devices
    capacity = 3 * toks * picks // (2 * experts)
    places = devices // GROUP
    step_of = float(local * GROUP)
    half = width // 2
    member = lax.axis_index("dp")
    swapped = functools.partial(swap, devices=devices)

    def mine(value, size, dim, flip=False):
        index = 1 - member if flip else member
        return lax.dynamic_slice_in_dim(value, index * size, size, dim)

    def after(value, *others):
        return lax.optimization_barrier((value, *others))[0]

    def kept_half(weight):
        return mine(weight, 1, 0)[0]

    def in_pieces(sent, pieces):
        size = sent.shape[0] // pieces
        return [swapped(sent[i * size : (i + 1) * size], across=1) for i in range(pieces)]

    def got_half(weight, pieces):
        return in_pieces(mine(weight, 1, 0, flip=True)[0], pieces)

    gate_pieces = got_half(gate_weight, 4)
    up_pieces = got_half(up_weight, 2)
    w_gate = kept_half(gate_weight), jnp.concatenate(gate_pieces)
    w_up = kept_half(up_weight), jnp.concatenate(up_pieces)
    w_down = kept_half(down_weight), got_half(down_weight, 1)[0]

    def z_rows(columns, across):
        return swapped(jnp.concatenate([tokens[:, columns], cotangent[:, columns]]), across=across, within=Z)

    table = jnp.concatenate([routing.T.astype(F32), route_gates.T], axis=0)
    near_table = jnp.stack([table, swapped(table, within=Z)])
    left, right = z_rows(slice(0, half), 0), z_rows(slice(half, width), 1)
    near_x = jnp.concatenate([tokens, jnp.concatenate([left[:toks], right[:toks]], axis=1)])
    near_c = jnp.concatenate([cotangent, jnp.concatenate([left[toks:], right[toks:]], axis=1)])
    near_x = after(near_x, near_table, gate_pieces[0])
    far_x, far_c = swapped(near_x, within=CORE), swapped(near_c, within=CORE)
    all_tables = jnp.concatenate([near_table, swapped(near_table, within=CORE)], axis=0)
    offset = (lax.axis_index("expert") % GROUP) * local + member
    keys = all_tables[:, :picks].reshape(GROUP * picks, toks) - offset.astype(F32)
    gates = all_tables[:, picks:].reshape(GROUP * picks, toks)

    sent_rows, place = pack_rows(keys, near_x, far_x, capacity, places, step_of)
    x = exchange(after(sent_rows, gate_pieces[1]), devices)
    sent_back, high, low = pack_back(
        after(keys, *gate_pieces[2:]), gates, place, near_c, far_c, capacity, places, step_of
    )
    back = exchange(after(sent_back, up_pieces[0]), devices)
    x = after(x, up_pieces[1])

    hidden, saved = [], []
    for j in range(2):
        gate_pre = dot(x, w_gate[j])
        up_pre = dot(x, w_up[j])
        s = jax.nn.sigmoid(gate_pre)
        active = gate_pre * s
        hidden.append((active * up_pre).astype(BF))
        saved.append((gate_pre, up_pre, s, active))
    out = (dot(hidden[0], w_down[0], NT) + dot(hidden[1], w_down[1], NT)).astype(BF)

    def outer(rows, values):
        return dot(rows, values, TN).astype(BF)

    def inner(j, back):
        gate_pre, up_pre, s, active = saved[j]
        dhidden = dot(back, w_down[j])
        d_gate = (dhidden * up_pre * s * (1.0 + gate_pre * (1.0 - s))).astype(BF)
        return d_gate, (dhidden * active).astype(BF)

    def partner(value):
        return swapped(value, across=1)

    back = after(back, out)
    sent_down = outer(back, hidden[1])
    got_out = exchange(after(out, sent_down), devices)
    d_gate1, d_up1 = inner(1, after(back, sent_down))
    sent_gate, sent_up = outer(x, d_gate1), outer(x, d_up1)
    d_gate0, d_up0 = inner(0, after(back, sent_gate, sent_up))
    row = (
        dot(d_gate0, w_gate[0], NT)
        + dot(d_up0, w_up[0], NT)
        + dot(d_gate1, w_gate[1], NT)
        + dot(d_up1, w_up[1], NT)
    ).astype(BF)
    got_down, got_gate = partner(sent_down), partner(sent_gate)
    most = 3 * width // 4
    up_first, up_rest = partner(sent_up[:most]), partner(sent_up[most:])
    got_row = exchange(after(row, got_out, got_down), devices)

    def over_core(kept, sent):
        return kept + swapped(sent, within=CORE).astype(F32)

    def spread(*kept):
        same = [mine(k, half, 1) for k in kept]
        cross = [mine(k, half, 1, flip=True) for k in kept]
        own = jnp.concatenate([c[:toks] for c in cross]).astype(BF)
        away = jnp.concatenate([c[toks:] for c in cross]).astype(BF)
        straight = jnp.concatenate([c[toks:] for c in same]).astype(BF)
        got = [swapped(straight, within=Z), swapped(away, across=1, within=Z), partner(own)]
        return [c[:toks] for c in same], got

    def collect(own, got):
        return (own + sum(g.astype(F32) for g in got)).astype(BF)

    def both(kept, got):
        first = iota((local, 1, 1), 0) == member
        return jnp.where(first, kept[None], got[None])

    mixed_kept, mixed_sent, gates_part = mix(
        keys, place, high, low, near_c, far_c, after(got_out, got_gate), capacity, places, step_of
    )
    down_grad = both(outer(after(back, mixed_kept), hidden[0]), got_down)
    gate_grad = both(outer(after(x, mixed_kept), d_gate0), got_gate)
    kept_up = outer(after(x, mixed_kept), d_up0)
    mixed_sum = over_core(mixed_kept, mixed_sent)
    got_row = after(got_row, down_grad, gate_grad, kept_up, up_first)
    (mixed_own, token_own), got = spread(mixed_sum, over_core(*sum_rows(place, got_row)))
    mixed = collect(mixed_own, [g[:toks] for g in got])
    token_grad = collect(token_own, [g[toks:] for g in got])
    up_grad = both(kept_up, jnp.concatenate([up_first, after(up_rest, token_grad)]))

    gates_near = gates_part[: 2 * picks] + swapped(gates_part[2 * picks :], within=CORE)
    own, away = gates_near[:picks], gates_near[picks:]
    gates_got = [partner(own), swapped(away, within=Z), swapped(away, across=1, within=Z)]
    gates_got = [after(g, token_own) for g in gates_got]
    gates_sum = (own + gates_got[0]) + (gates_got[1] + gates_got[2])
    return mixed, token_grad, gates_sum.T, gate_grad, up_grad, down_grad


def solution(mesh):
    by_dp = P("expert", None, "dp")
    rows = P("expert", None)
    in_specs = (rows, rows, rows, by_dp, by_dp, by_dp, rows)
    out_specs = (P("expert", "dp"), P("expert", "dp"), rows, by_dp, by_dp, by_dp)
    return jax.shard_map(body, mesh=mesh, in_specs=in_specs, out_specs=out_specs, check_vma=False)
```

```python
import functools

import jax
import jax.numpy as jnp
from jax import lax
from jax.experimental import pallas as pl
from jax.experimental.pallas import tpu as pltpu
from jax.sharding import PartitionSpec as P

BF = jnp.bfloat16
F32 = jnp.float32
NN = (((1,), (0,)), ((), ()))
TN = (((0,), (0,)), ((), ()))
NT = (((1,), (1,)), ((), ()))
LIMIT = 48 * 2**20
PACK_LIMIT = 60 * 2**20
GROUP = 4
EXACT = lax.Precision.HIGHEST


def dot(a, b, dims=NN, precision=None):
    return lax.dot_general(a, b, dims, precision=precision, preferred_element_type=F32)


def iota(shape, dim):
    return lax.broadcasted_iota(jnp.int32, shape, dim)


def as_float(flags):
    return flags.astype(F32)


def slot_parts(first, rows, cols, capacity):
    slot = as_float(first + iota((rows, cols), 0))
    place = jnp.floor((slot + 0.5) * (1.0 / (GROUP * capacity)))
    rest = slot - GROUP * capacity * place
    block = jnp.floor((rest + 0.5) * (1.0 / capacity))
    return place, block, rest - capacity * block


def one_hot_pair(first, rows, places, capacity):
    place, block, _ = slot_parts(first, rows, GROUP * places, capacity)
    return as_float(as_float(iota((rows, GROUP * places), 1)) == block * places + place)


def by_pair(keys_ref, value, places, step=8.0):
    toks = keys_ref.shape[1]
    picks = keys_ref.shape[0] // GROUP
    wanted = as_float(iota((places, toks), 0)) * step
    blocks = []
    for b in range(GROUP):
        total = jnp.zeros((places, toks), F32)
        for k in range(picks):
            row = b * picks + k
            total += jnp.where(keys_ref[row : row + 1, :] == wanted, value(row), 0.0)
        blocks.append(total)
    return jnp.concatenate(blocks, axis=0)


def pack_rows_kernel(capacity, step_of, keys_ref, near_ref, far_ref, rows_ref, place_ref, rank_ref):
    step = pl.program_id(0)
    pairs, toks = rank_ref.shape
    places = pairs // GROUP
    rows = rows_ref.shape[0]

    @pl.when(step == 0)
    def _():
        named = by_pair(keys_ref, lambda row: 1.0, places, step_of)
        before = as_float(iota((toks, toks), 0) < iota((toks, toks), 1)).astype(BF)
        rank = dot(named.astype(BF), before)
        rank_ref[...] = jnp.where(named > 0, rank, -1.0).astype(BF)

    first = step * rows
    pair = one_hot_pair(first, rows, places, capacity).astype(BF)
    _, block, rank = slot_parts(first, rows, toks, capacity)
    hit = dot(pair, rank_ref[...]) == rank
    place = jnp.concatenate(
        [as_float(hit & (block == float(b))) for b in range(GROUP)], axis=1
    ).astype(BF)
    place_ref[...] = place
    half = near_ref.shape[0]
    rows_ref[...] = (
        dot(place[:, :half], near_ref[...]) + dot(place[:, half:], far_ref[...])
    ).astype(BF)


def pack_rows(keys, near, far, capacity, places, step_of, steps=2):
    toks = keys.shape[1]
    width = near.shape[1]
    slots = places * GROUP * capacity
    rows = slots // steps
    whole = lambda i: (0, 0)
    part = lambda i: (i, 0)
    return pl.pallas_call(
        functools.partial(pack_rows_kernel, capacity, step_of),
        grid=(steps,),
        in_specs=[pl.BlockSpec(a.shape, whole) for a in (keys, near, far)],
        out_specs=[
            pl.BlockSpec((rows, width), part),
            pl.BlockSpec((rows, GROUP * toks), part),
        ],
        out_shape=[
            jax.ShapeDtypeStruct((slots, width), BF),
            jax.ShapeDtypeStruct((slots, GROUP * toks), BF),
        ],
        scratch_shapes=[pltpu.VMEM((GROUP * places, toks), BF)],
        compiler_params=pltpu.CompilerParams(vmem_limit_bytes=PACK_LIMIT),
        cost_estimate=pl.CostEstimate(
            flops=8 * slots * toks * width, bytes_accessed=2 * slots * width, transcendentals=0
        ),
        name="pack_rows",
    )(keys, near, far)


def pack_back_kernel(capacity, step_of, keys_ref, gates_ref, place_ref, near_ref, far_ref, rows_ref, high_ref, low_ref, by_ref):
    step = pl.program_id(0)
    pairs, toks = by_ref.shape
    places = pairs // GROUP
    rows = rows_ref.shape[0]

    @pl.when(step == 0)
    def _():
        by_ref[...] = by_pair(keys_ref, lambda row: gates_ref[row : row + 1, :], places, step_of)

    pair = one_hot_pair(step * rows, rows, places, capacity)
    gate = dot(pair, by_ref[...], precision=EXACT)
    place = place_ref[...]
    weight = as_float(place) * jnp.concatenate([gate] * GROUP, axis=1)
    high = weight.astype(BF)
    high_ref[...] = high
    low_ref[...] = (weight - as_float(high)).astype(BF)
    scale = jnp.sum(weight, axis=1, keepdims=True)
    half = near_ref.shape[0]
    cot = dot(place[:, :half], near_ref[...]) + dot(place[:, half:], far_ref[...])
    rows_ref[...] = (scale * cot).astype(BF)


def pack_back(keys, gates, place, near, far, capacity, places, step_of, steps=2):
    toks = keys.shape[1]
    width = near.shape[1]
    slots = places * GROUP * capacity
    rows = slots // steps
    whole = lambda i: (0, 0)
    part = lambda i: (i, 0)
    return pl.pallas_call(
        functools.partial(pack_back_kernel, capacity, step_of),
        grid=(steps,),
        in_specs=[
            pl.BlockSpec(keys.shape, whole),
            pl.BlockSpec(gates.shape, whole),
            pl.BlockSpec((rows, GROUP * toks), part),
            pl.BlockSpec(near.shape, whole),
            pl.BlockSpec(far.shape, whole),
        ],
        out_specs=[
            pl.BlockSpec((rows, width), part),
            pl.BlockSpec((rows, GROUP * toks), part),
            pl.BlockSpec((rows, GROUP * toks), part),
        ],
        out_shape=[
            jax.ShapeDtypeStruct((slots, width), BF),
            jax.ShapeDtypeStruct((slots, GROUP * toks), BF),
            jax.ShapeDtypeStruct((slots, GROUP * toks), BF),
        ],
        scratch_shapes=[pltpu.VMEM((GROUP * places, toks), F32)],
        compiler_params=pltpu.CompilerParams(vmem_limit_bytes=PACK_LIMIT),
        cost_estimate=pl.CostEstimate(
            flops=8 * slots * toks * width, bytes_accessed=2 * slots * width, transcendentals=0
        ),
        name="pack_back",
    )(keys, gates, place, near, far)


def mix_kernel(capacity, places, step_of, keys_ref, place_ref, high_ref, low_ref, near_ref, far_ref, rows_ref, kept_ref, sent_ref, gates_ref, along_ref):
    step = pl.program_id(0)
    rows = rows_ref[...]
    half = near_ref.shape[0]
    mixed = dot(high_ref[...], rows, TN) + dot(low_ref[...], rows, TN)
    kept_ref[...] = mixed[:half]
    sent_ref[...] = mixed[half:].astype(BF)

    @pl.when(step == 0)
    def _():
        along_ref[...] = jnp.zeros_like(along_ref)

    along_ref[:, :half] += dot(rows, near_ref[...], NT)
    along_ref[:, half:] += dot(rows, far_ref[...], NT)

    @pl.when(step == pl.num_programs(0) - 1)
    def _():
        slots = along_ref.shape[0]
        toks = keys_ref.shape[1]
        picks = keys_ref.shape[0] // GROUP
        kept = along_ref[...] * as_float(place_ref[...])
        kept = sum(kept[:, b * toks : (b + 1) * toks] for b in range(GROUP))
        by = dot(one_hot_pair(0, slots, places, capacity), kept, TN, precision=EXACT)
        wanted = as_float(iota((places, toks), 0)) * step_of
        for b in range(GROUP):
            mine = by[b * places : (b + 1) * places, :]
            for k in range(picks):
                row = b * picks + k
                chosen = jnp.where(keys_ref[row : row + 1, :] == wanted, mine, 0.0)
                gates_ref[row : row + 1, :] = jnp.sum(chosen, axis=0, keepdims=True)


def mix(keys, place, high, low, near, far, rows, capacity, places, step_of, steps=4):
    slots, all_toks = place.shape
    width = rows.shape[1]
    cols = width // steps
    whole = lambda i: (0, 0)
    part = lambda i: (0, i)
    return pl.pallas_call(
        functools.partial(mix_kernel, capacity, places, step_of),
        grid=(steps,),
        in_specs=[pl.BlockSpec(a.shape, whole) for a in (keys, place, high, low)]
        + [pl.BlockSpec((a.shape[0], cols), part) for a in (near, far, rows)],
        out_specs=[pl.BlockSpec((all_toks // 2, cols), part)] * 2 + [pl.BlockSpec(keys.shape, whole)],
        out_shape=[
            jax.ShapeDtypeStruct((all_toks // 2, width), F32),
            jax.ShapeDtypeStruct((all_toks // 2, width), BF),
            jax.ShapeDtypeStruct(keys.shape, F32),
        ],
        scratch_shapes=[pltpu.VMEM((slots, all_toks), F32)],
        compiler_params=pltpu.CompilerParams(vmem_limit_bytes=LIMIT),
        cost_estimate=pl.CostEstimate(
            flops=6 * slots * all_toks * width, bytes_accessed=2 * slots * width, transcendentals=0
        ),
        name="mix",
    )(keys, place, high, low, near, far, rows)


def sum_rows_kernel(place_ref, rows_ref, kept_ref, sent_ref):
    total = dot(place_ref[...], rows_ref[...], TN)
    half = kept_ref.shape[0]
    kept_ref[...] = total[:half]
    sent_ref[...] = total[half:].astype(BF)


def sum_rows(place, rows, steps=4):
    slots, toks = place.shape
    width = rows.shape[1]
    cols = width // steps
    return pl.pallas_call(
        sum_rows_kernel,
        grid=(steps,),
        in_specs=[
            pl.BlockSpec((slots, toks), lambda i: (0, 0)),
            pl.BlockSpec((slots, cols), lambda i: (0, i)),
        ],
        out_specs=[pl.BlockSpec((toks // 2, cols), lambda i: (0, i))] * 2,
        out_shape=[
            jax.ShapeDtypeStruct((toks // 2, width), F32),
            jax.ShapeDtypeStruct((toks // 2, width), BF),
        ],
        compiler_params=pltpu.CompilerParams(vmem_limit_bytes=LIMIT),
        cost_estimate=pl.CostEstimate(
            flops=2 * slots * toks * width, bytes_accessed=2 * slots * width, transcendentals=0
        ),
        name="sum_rows",
    )(place, rows)


def exchange(rows, devices):
    groups = [list(range(g, devices, GROUP)) for g in range(GROUP)]
    return lax.all_to_all(
        rows, "expert", split_axis=0, concat_axis=0, tiled=True, axis_index_groups=groups
    )


def swap(value, devices, across=0, within=0):
    pairs = [
        (m * devices + s, (m ^ across) * devices + (s ^ within)) for m in range(2) for s in range(devices)
    ]
    return lax.ppermute(value, ("dp", "expert"), pairs)


CORE, Z = 1, 2


def body(tokens, routing, route_gates, gate_weight, up_weight, down_weight, cotangent):
    toks, width = tokens.shape
    picks = routing.shape[1]
    local = gate_weight.shape[0]
    devices = lax.axis_size("expert")
    experts = local * devices
    capacity = 3 * toks * picks // (2 * experts)
    places = devices // GROUP
    step_of = float(local * GROUP)
    half = width // 2
    member = lax.axis_index("dp")
    swapped = functools.partial(swap, devices=devices)

    def mine(value, size, dim, flip=False):
        index = 1 - member if flip else member
        return lax.dynamic_slice_in_dim(value, index * size, size, dim)

    def after(value, *others):
        return lax.optimization_barrier((value, *others))[0]

    def kept_half(weight):
        return mine(weight, 1, 0)[0]

    def in_pieces(sent, pieces):
        size = sent.shape[0] // pieces
        return [swapped(sent[i * size : (i + 1) * size], across=1) for i in range(pieces)]

    def got_half(weight, pieces):
        return in_pieces(mine(weight, 1, 0, flip=True)[0], pieces)

    gate_pieces = got_half(gate_weight, 4)
    up_pieces = got_half(up_weight, 2)
    w_gate = kept_half(gate_weight), jnp.concatenate(gate_pieces)
    w_up = kept_half(up_weight), jnp.concatenate(up_pieces)
    w_down = kept_half(down_weight), got_half(down_weight, 1)[0]

    def z_rows(columns, across):
        return swapped(jnp.concatenate([tokens[:, columns], cotangent[:, columns]]), across=across, within=Z)

    table = jnp.concatenate([routing.T.astype(F32), route_gates.T], axis=0)
    near_table = jnp.stack([table, swapped(table, within=Z)])
    left, right = z_rows(slice(0, half), 0), z_rows(slice(half, width), 1)
    near_x = jnp.concatenate([tokens, jnp.concatenate([left[:toks], right[:toks]], axis=1)])
    near_c = jnp.concatenate([cotangent, jnp.concatenate([left[toks:], right[toks:]], axis=1)])
    near_x = after(near_x, near_table, gate_pieces[0])
    far_x, far_c = swapped(near_x, within=CORE), swapped(near_c, within=CORE)
    all_tables = jnp.concatenate([near_table, swapped(near_table, within=CORE)], axis=0)
    offset = (lax.axis_index("expert") % GROUP) * local + member
    keys = all_tables[:, :picks].reshape(GROUP * picks, toks) - offset.astype(F32)
    gates = all_tables[:, picks:].reshape(GROUP * picks, toks)

    sent_rows, place = pack_rows(keys, near_x, far_x, capacity, places, step_of)
    x = exchange(after(sent_rows, gate_pieces[1]), devices)
    sent_back, high, low = pack_back(
        after(keys, *gate_pieces[2:]), gates, place, near_c, far_c, capacity, places, step_of
    )
    back = exchange(after(sent_back, up_pieces[0]), devices)
    x = after(x, up_pieces[1])

    hidden, saved = [], []
    for j in range(2):
        gate_pre = dot(x, w_gate[j])
        up_pre = dot(x, w_up[j])
        s = jax.nn.sigmoid(gate_pre)
        active = gate_pre * s
        hidden.append((active * up_pre).astype(BF))
        saved.append((gate_pre, up_pre, s, active))
    out = (dot(hidden[0], w_down[0], NT) + dot(hidden[1], w_down[1], NT)).astype(BF)

    def outer(rows, values):
        return dot(rows, values, TN).astype(BF)

    def inner(j, back):
        gate_pre, up_pre, s, active = saved[j]
        dhidden = dot(back, w_down[j])
        d_gate = (dhidden * up_pre * s * (1.0 + gate_pre * (1.0 - s))).astype(BF)
        return d_gate, (dhidden * active).astype(BF)

    def partner(value):
        return swapped(value, across=1)

    back = after(back, out)
    sent_down = outer(back, hidden[1])
    got_out = exchange(after(out, sent_down), devices)
    d_gate1, d_up1 = inner(1, after(back, sent_down))
    sent_gate, sent_up = outer(x, d_gate1), outer(x, d_up1)
    d_gate0, d_up0 = inner(0, after(back, sent_gate, sent_up))
    row = (
        dot(d_gate0, w_gate[0], NT)
        + dot(d_up0, w_up[0], NT)
        + dot(d_gate1, w_gate[1], NT)
        + dot(d_up1, w_up[1], NT)
    ).astype(BF)
    got_down, got_gate, got_up = partner(sent_down), partner(sent_gate), partner(sent_up)
    got_row = exchange(after(row, got_out, got_down), devices)

    def over_core(kept, sent):
        return kept + swapped(sent, within=CORE).astype(F32)

    def spread(*kept):
        same = [mine(k, half, 1) for k in kept]
        cross = [mine(k, half, 1, flip=True) for k in kept]
        own = jnp.concatenate([c[:toks] for c in cross]).astype(BF)
        away = jnp.concatenate([c[toks:] for c in cross]).astype(BF)
        straight = jnp.concatenate([c[toks:] for c in same]).astype(BF)
        got = [swapped(straight, within=Z), swapped(away, across=1, within=Z), partner(own)]
        return [c[:toks] for c in same], got

    def collect(own, got):
        return (own + sum(g.astype(F32) for g in got)).astype(BF)

    def both(kept, got):
        first = iota((local, 1, 1), 0) == member
        return jnp.where(first, kept[None], got[None])

    mixed_kept, mixed_sent, gates_part = mix(
        keys, place, high, low, near_c, far_c, after(got_out, got_gate), capacity, places, step_of
    )
    down_grad = both(outer(after(back, mixed_kept), hidden[0]), got_down)
    gate_grad = both(outer(after(x, mixed_kept), d_gate0), got_gate)
    kept_up = outer(after(x, mixed_kept), d_up0)
    mixed_sum = over_core(mixed_kept, mixed_sent)
    got_row = after(got_row, down_grad, gate_grad, kept_up, got_up)
    (mixed_own, token_own), got = spread(mixed_sum, over_core(*sum_rows(place, got_row)))
    mixed = collect(mixed_own, [g[:toks] for g in got])
    token_grad = collect(token_own, [g[toks:] for g in got])
    up_grad = both(kept_up, got_up)

    gates_near = gates_part[: 2 * picks] + swapped(gates_part[2 * picks :], within=CORE)
    own, away = gates_near[:picks], gates_near[picks:]
    gates_got = [partner(own), swapped(away, within=Z), swapped(away, across=1, within=Z)]
    gates_got = [after(g, token_own) for g in gates_got]
    gates_sum = (own + gates_got[0]) + (gates_got[1] + gates_got[2])
    return mixed, token_grad, gates_sum.T, gate_grad, up_grad, down_grad


def solution(mesh):
    by_dp = P("expert", None, "dp")
    rows = P("expert", None)
    in_specs = (rows, rows, rows, by_dp, by_dp, by_dp, rows)
    out_specs = (P("expert", "dp"), P("expert", "dp"), rows, by_dp, by_dp, by_dp)
    return jax.shard_map(body, mesh=mesh, in_specs=in_specs, out_specs=out_specs, check_vma=False)
```
